256 devices in a mesh: lon: 32 (over z, x), lat: 2 (over core), lev: 4 (over y).
Axes of the slice: x: 4, y: 4, z: 8, core: 2. Of those that a mesh axis runs over, the one named last changes fastest.
Arguments:
- state: float32 [6, 8, 1152, 768], P(None, 'lev', 'lon', 'lat'), may hold values from -6 to 6
- east_courant: float32 [8, 1152, 768], P('lev', 'lon', 'lat'), may hold values from -0.2 to 0.2
- north_courant: float32 [8, 1152, 768], P('lev', 'lon', 'lat'), may hold values from -0.2 to 0.2
- cutoff: int32 [768], replicated, may hold values from 4 to 576
Outputs:
- advanced: float32 [6, 8, 1152, 768], P(None, 'lev', 'lon', 'lat')
The draws below stay inside these ranges and needn't reach their ends.
Inputs may be any that keep to these rules, and one draw needn't show every extreme that they name: `cutoff`: only the entries of the first 96 and the last 96 rows are read.
All inputs are finite; a program needn't handle non-finite values.
Results may differ from the reference program's by a relative error of at most 0.0001.
Values sent between devices are 32-bit elements; how exact they have to be, the bound alone decides.
No kernel may reach another device: no remote copies, remote signals or barrier semaphores. Data moves between devices by JAX's collectives and lax.ppermute only.
A program may use at most 128 MiB of HBM per device.

```python
import jax
import jax.numpy as jnp

FIELDS = 6
NLON = 1152
NK = 577
NLEV = 8
NLAT = 768
POLAR = 96
SUBSTEPS = 2


def set_ends(values, rng, least, largest):
    index_at = [jax.random.randint(jax.random.fold_in(rng, axis), (), 0, length) for axis, length in enumerate(values.shape)]
    widest = values.shape.index(max(values.shape))
    neighbour = index_at[:widest] + [(index_at[widest] + 1) % values.shape[widest]] + index_at[widest + 1:]
    return values.at[tuple(index_at)].set(least).at[tuple(neighbour)].set(largest)


def block_scale(rng, dims, pieces, smallest, top_value):
    level = 1.0
    for axis_at, shards_of in pieces:
        heights = jax.random.uniform(jax.random.fold_in(jax.random.fold_in(rng, 6), axis_at), (shards_of,), jnp.float32, smallest / len(pieces), top_value / len(pieces))
        level = level * jnp.repeat(jnp.exp(heights), dims[axis_at] // shards_of).reshape((-1,) + (1,) * (len(dims) - 1 - axis_at))
    return level


def scatter_about(key, extent, scale, limit, cuts=(), kind=jnp.bfloat16):
    entries = jax.random.normal(key, extent, jnp.float32) * scale
    if len(cuts) > 0:
        entries = block_scale(key, extent, cuts, -0.22, 0.18) * entries
    return jnp.clip(entries, min=-limit, max=limit).astype(kind)


def setup_inputs(seed: int = 0) -> dict:
    splits = jax.random.split(jax.random.key(seed), 5)
    state = scatter_about(splits[0], (FIELDS, NLEV, NLON, NLAT), 1.0, 6.0, ((1, 4), (2, 32), (3, 2)), jnp.float32)
    east_courant = jnp.clip(jax.random.uniform(splits[1], (NLEV, NLON, NLAT), jnp.float32, -0.2, 0.2) * block_scale(splits[1], (NLEV, NLON, NLAT), ((0, 4), (1, 32), (2, 2)), -0.4, 0.0), -0.2, 0.2)
    north_courant = jnp.clip(jax.random.uniform(splits[2], (NLEV, NLON, NLAT), jnp.float32, -0.2, 0.2) * block_scale(splits[2], (NLEV, NLON, NLAT), ((0, 4), (1, 32), (2, 2)), -0.4, 0.0), -0.2, 0.2)
    cutoff = set_ends(jax.random.randint(splits[3], (NLAT,), 4, NK), jax.random.fold_in(splits[3], 1), 4, NK - 1).astype(jnp.int32)
    return dict(state=state, east_courant=east_courant, north_courant=north_courant, cutoff=cutoff)


def substep(state, east_courant, north_courant):
    west = jnp.roll(state, 1, axis=3)
    east = jnp.roll(state, -1, axis=3)
    across = jnp.roll(state, NLON // 2, axis=3)
    south = jnp.concatenate([across[:, :, :1], state[:, :, :-1]], axis=2)
    north = jnp.concatenate([state[:, :, 1:], across[:, :, -1:]], axis=2)
    east_face = jnp.roll(east_courant, -1, axis=2)
    row_ids = jnp.arange(NLAT, dtype=jnp.int32)
    north_face = jnp.where((row_ids == NLAT - 1)[None, :, None], 0.0, north_courant)
    south_face = jnp.concatenate([jnp.zeros_like(north_face[:, :1]), north_face[:, :-1]], axis=1)
    flux_west = jnp.maximum(east_courant, 0.0) * west + jnp.minimum(east_courant, 0.0) * state
    flux_east = jnp.maximum(east_face, 0.0) * state + jnp.minimum(east_face, 0.0) * east
    flux_south = jnp.maximum(south_face, 0.0) * south + jnp.minimum(south_face, 0.0) * state
    flux_north = jnp.maximum(north_face, 0.0) * state + jnp.minimum(north_face, 0.0) * north
    spread = west + east + south + north - 4.0 * state
    return state + flux_west - flux_east + flux_south - flux_north + 0.125 * spread


def polar_filter(state, cutoff):
    rows = jnp.concatenate([state[:, :, :POLAR], state[:, :, NLAT - POLAR:]], axis=2)
    cuts = jnp.concatenate([cutoff[:POLAR], cutoff[NLAT - POLAR:]])
    keep = jnp.arange(NK, dtype=jnp.int32)[None, :] <= cuts[:, None]
    spectrum = jnp.fft.rfft(rows, axis=3)
    spectrum = jnp.where(keep[None, None], spectrum, 0.0)
    smooth = jnp.fft.irfft(spectrum, n=NLON, axis=3).astype(state.dtype)
    middle = state[:, :, POLAR:NLAT - POLAR]
    return jnp.concatenate([smooth[:, :, :POLAR], middle, smooth[:, :, POLAR:]], axis=2)


def reference(state, east_courant, north_courant, cutoff):
    state = jnp.swapaxes(state, 2, 3)
    east_courant = jnp.swapaxes(east_courant, 1, 2)
    north_courant = jnp.swapaxes(north_courant, 1, 2)
    for step in range(SUBSTEPS):
        state = substep(state, east_courant, north_courant)
        state = polar_filter(state, cutoff)
    return jnp.swapaxes(state, 2, 3)
```

```python
import math

import jax
import jax.numpy as jnp
import numpy as np
from jax import lax
from jax.experimental import pallas as pl
from jax.experimental.layout import Layout, with_layout_constraint
from jax.experimental.pallas import tpu as pltpu
from jax.sharding import PartitionSpec as P

FIELDS = 6
UNITS = 8
NLON = 1152
HALF = NLON // 2
QUARTER = NLON // 4
NLAT = 768
POLAR = 96
LEVELS = 2
LON = 36
LAT = 384
RING = 32
GROUPS = 16
SHARE = 6
SPAN = 10
SLOT = 7
KAPPA = 0.125
BLOCK = 64
PIECE = 48
TILES = LAT // 128
STEP = TILES * LEVELS
UNIT = LON * STEP
EDGE = 2 * STEP + 2 * LEVELS
ORDER = Layout(major_to_minor=(0, 1, 3, 2, 4))


def lanes_of(rows, width=128):
    return lax.broadcasted_iota(jnp.int32, (rows, width), 1)


def pick(flag, rows, width, yes, no):
    return jnp.where(jnp.full((rows, width), flag, jnp.int32) == 0, yes, no)


def to_rows(x):
    units = x.size // (LEVELS * LON * LAT)
    x = x.reshape(units, LEVELS, LON, LAT).transpose(0, 2, 1, 3)
    x = with_layout_constraint(x.reshape(units, LON, LEVELS, TILES, 128), ORDER)
    return x.transpose(0, 1, 3, 2, 4).reshape(units * UNIT, 128)


def from_rows(x):
    x = x.reshape(FIELDS, LON, TILES, LEVELS, 128).transpose(0, 1, 3, 2, 4)
    x = with_layout_constraint(x, ORDER)
    return x.reshape(FIELDS, LON, LEVELS, LAT).transpose(0, 2, 1, 3)


def unit(state, cx, cy, u):
    return (state, u * UNIT) if u < FIELDS else ((cx, cy)[u - FIELDS], 0)


def part(ref, start, level, tile, first, count):
    return ref[pl.ds(start + first * STEP + tile * LEVELS + level, count, stride=STEP), :]


def on_core(body):
    lat = lax.axis_index("lat")
    for n in range(2):
        pl.when(lat == n)(lambda n=n: body(n))


def pack_kernel(state, cx, cy, chunks_out, window_out, edge_out, block, tails, slots, chunks, window, edge, sems):
    loads = []
    for u in range(UNITS):
        ref, start = unit(state, cx, cy, u)
        loads.append(pltpu.make_async_copy(ref.at[start:start + UNIT], block.at[u * UNIT:u * UNIT + UNIT], sems.at[u]))
    for copy in loads:
        copy.start()
    sends = [
        pltpu.make_async_copy(window, window_out, sems.at[UNITS]),
        pltpu.make_async_copy(edge, edge_out, sems.at[UNITS + 1]),
    ]
    for n in range(4):
        some = pl.ds(n * RING // 4, RING // 4)
        sends.append(pltpu.make_async_copy(chunks.at[some], chunks_out.at[some], sems.at[UNITS + 2 + n]))
    lane = lanes_of(8)

    def body(lat):
        for u in range(UNITS):
            loads[u].wait()
            start = u * UNIT
            edge[EDGE * u:EDGE * u + EDGE] = block[start:start + EDGE]
            at = EDGE * (UNITS + u)
            edge[at:at + 12] = block[start + UNIT - 12:start + UNIT]
            edge[at + 12:at + EDGE] = block[start + UNIT - 4:start + UNIT]
            for level in range(LEVELS):
                rows = pl.ds(2 * LON * u + level, LON, stride=LEVELS)
                window[rows, :] = part(block, start, level, 2 - 2 * lat, 0, LON)
                main = part(block, start, level, 2 * lat, 0, 24)
                slots[level, u] = pltpu.roll(main, (SPAN * u - 32 * lat) % 128, 1)
                row = 12 * (u // 4)
                tails[level, u % 4, row:row + 12] = part(block, start, level, 2 * lat, 24, 12)
        sends[0].start()
        sends[1].start()
        for level in range(LEVELS):
            for at in range(4):
                slots[level, 8 + at] = pltpu.roll(tails[level, at], (SPAN * (8 + at) - 32 * lat) % 128, 1)
            for g in range(GROUPS):
                first = SHARE * g - 2
                begins = sorted(((first + SPAN * n) % 128, n) for n in range(12))
                for k in range(0, 24, 8):
                    value = slots[level, begins[-1][1], k:k + 8]
                    for begin, n in begins:
                        value = jnp.where(lane >= begin, slots[level, n, k:k + 8], value)
                    chunks[level * GROUPS + g, k:k + 8] = value
                if g % 8 == 7:
                    sends[2 + level * 2 + g // 8].start()

    on_core(body)
    for copy in sends:
        copy.wait()


def edge_kernel(edge, window, head, tail):
    head[...] = edge[:EDGE * UNITS]
    tail[...] = edge[EDGE * UNITS:]
    for u in range(UNITS):
        at, beyond = EDGE * u, 2 * LON * u
        head[at + 12:at + EDGE] = window[beyond:beyond + 4]
        tail[at + 12:at + EDGE] = window[beyond + 2 * LON - 4:beyond + 2 * LON]


def limit_kernel(head, table, cutoff, limits):
    del head, table
    low = lax.axis_index("lat") * (NLAT - POLAR) + SHARE * lax.rem(lax.axis_index("lon"), GROUPS) - 2
    row = lanes_of(8) % SPAN
    found = jnp.zeros((8, 128), jnp.int32)
    for r in range(SPAN):
        found = jnp.where(row == r, cutoff[jnp.clip(low + r, 0, NLAT - 1)], found)
    limits[...] = found


def coefficients(cx, cx_east, cy_south, cy_north):
    west = jnp.maximum(cx, 0.0) + KAPPA
    east = KAPPA - jnp.minimum(cx_east, 0.0)
    south = jnp.maximum(cy_south, 0.0) + KAPPA
    north = KAPPA - jnp.minimum(cy_north, 0.0)
    centre = (
        (1.0 - 4.0 * KAPPA)
        + (jnp.minimum(cx, 0.0) - jnp.maximum(cx_east, 0.0))
        + (jnp.minimum(cy_south, 0.0) - jnp.maximum(cy_north, 0.0))
    )
    return west, east, south, north, centre


def middle_kernel(state, cx, cy, west, east, window, out, weight, ext, coef):
    lat = lax.axis_index("lat")

    def extended(u, level):
        ref, start = unit(state, cx, cy, u)
        for t in range(TILES):
            ext[:LON, 128 * t:128 * t + 128] = part(ref, start, level, t, 0, LON)
            ext[LON:LON + 2, 128 * t:128 * t + 128] = part(east, EDGE * u, level, t, 0, 2)
            ext[LON + 2:, 128 * t:128 * t + 128] = part(west, EDGE * u, level, t, 0, 2)
        ext[:LON, LAT:] = window[pl.ds(2 * LON * u + level, LON, stride=LEVELS), :]
        ext[LON:LON + 2, LAT:] = east[pl.ds(EDGE * u + 12 + level, 2, stride=LEVELS), :]
        ext[LON + 2:, LAT:] = west[pl.ds(EDGE * u + 12 + level, 2, stride=LEVELS), :]
        return ext[...]

    lane = lanes_of(LON + 4, LAT + 128)
    edge = lane == jnp.where(lat == 0, POLAR - 1, LAT - POLAR)
    beside = lanes_of(LON + 4) == jnp.where(lat == 0, POLAR, 31)
    for level in range(LEVELS):
        cxe = extended(FIELDS, level)
        cye = extended(FIELDS + 1, level)
        parts = coefficients(cxe, pltpu.roll(cxe, LON + 3, 0), pltpu.roll(cye, 1, 1), cye)
        for n, value in enumerate(parts):
            coef[n] = value
        near = pick(lat, LON + 4, 128, parts[2][:, :128], parts[3][:, 256:LAT])
        weight[level * (LON + 4):(level + 1) * (LON + 4)] = jnp.where(beside, near, 0.0)

        def substep(q):
            return (
                coef[0] * pltpu.roll(q, 1, 0)
                + coef[1] * pltpu.roll(q, LON + 3, 0)
                + coef[2] * pltpu.roll(q, 1, 1)
                + coef[3] * pltpu.roll(q, LAT + 127, 1)
                + coef[4] * q
            )

        for u in range(FIELDS):
            once = jnp.where(edge, 0.0, substep(extended(u, level)))
            twice = substep(once)
            for t in range(TILES):
                rows = pl.ds(u * UNIT + t * LEVELS + level, LON, stride=STEP)
                out[rows, :] = twice[:LON, 128 * t:128 * t + 128]


def hartley_tables():
    def split(n, shift):
        at = 2 * np.arange(n, dtype=np.int64) + shift
        angle = 2.0 * np.pi / (4 * n) * (at[:, None] * at[None, :] % (4 * n))
        table = np.cos(angle) + np.sin(angle)
        high = table.astype(jnp.bfloat16)
        low = (table - high.astype(np.float64)).astype(jnp.bfloat16)
        return np.concatenate([high, low], axis=1)

    even = np.concatenate([split(QUARTER, 0), split(QUARTER, 1)], axis=0)
    return np.concatenate([split(HALF, 1), even], axis=1)


def circle_kernel(chunks, table, limits, west, east, out, back, q0, q1, coef, spread, *buffers):
    del west, east
    odd_in, even_in, rest_in, odd_out, even_out, rest_out, lanes_in, sems = buffers
    lat = lax.axis_index("lat")
    group = lax.rem(lax.axis_index("lon"), GROUPS)
    low = SHARE * group - 2
    lane24 = lanes_of(24)
    for i in range(RING):
        chunk = chunks[i]
        at = 8 + LON * i
        q0[at:at + 24] = pltpu.roll(chunk, (-low) & 127, 1)
        upper = pltpu.roll(chunk, (-low - 8 * SPAN) & 127, 1)
        lower = pltpu.roll(chunk, (-low - 4 * SPAN) & 127, 1)
        q0[at + 24:at + 36] = jnp.where(lane24[:12] < 4 * SPAN, upper[:12], lower[12:])
    q0[7:8] = q0[7 + NLON:8 + NLON]
    q0[8 + NLON:9 + NLON] = q0[8:9]

    row = lanes_of(BLOCK) % SPAN
    pole_south = (row == 2) & (jnp.full((BLOCK, 128), lat + group, jnp.int32) == 0)
    pole_north = (row == SPAN - 3) & (jnp.full((BLOCK, 128), lat * GROUPS + group, jnp.int32) == 2 * GROUPS - 1)

    def split(ref, at, x, again=0):
        rows = x.shape[0]
        high = x.astype(jnp.bfloat16)
        rest = (x - high.astype(jnp.float32)).astype(jnp.bfloat16)
        for begin in (at, at + again)[:2 if again else 1]:
            ref[begin:begin + rows, :128] = high
            ref[begin:begin + rows, 128:] = rest

    def moved(sources):
        at = lax.broadcasted_iota(jnp.int32, (128, 128), 0)
        places = [jnp.where(at == source, 1.0, 0.0).astype(jnp.bfloat16) for source in sources]
        places = jnp.concatenate(places, axis=1)
        return jnp.dot(lanes_in[...], jnp.concatenate([places] * 2, axis=0), preferred_element_type=jnp.float32)

    for b in range(0, NLON, PIECE):
        split(lanes_in, b, q0[8 + b:8 + b + PIECE])
    take_x = FIELDS * SPAN + lanes_of(128) % SPAN
    spread[:NLON] = moved((take_x, take_x + SPAN))
    spread[NLON:NLON + 8] = spread[:8]

    def substep(q, b, parts):
        across = q[8 + (b + HALF) % NLON:8 + (b + HALF) % NLON + BLOCK]
        here = q[8 + b:8 + b + BLOCK]
        return (
            parts[0] * q[7 + b:7 + b + BLOCK]
            + parts[1] * q[9 + b:9 + b + BLOCK]
            + parts[2] * jnp.where(pole_south, across, pltpu.roll(here, 1, 1))
            + parts[3] * jnp.where(pole_north, across, pltpu.roll(here, 127, 1))
            + parts[4] * here
        )

    for b in range(0, NLON, BLOCK):
        cy = spread[b:b + BLOCK, 128:]
        parts = coefficients(
            spread[b:b + BLOCK, :128],
            spread[b + 1:b + 1 + BLOCK, :128],
            jnp.where(pole_south, 0.0, pltpu.roll(cy, 1, 1)),
            jnp.where(pole_north, 0.0, cy),
        )
        for n, value in enumerate(parts):
            coef[n, b:b + BLOCK] = value
        q1[8 + b:8 + b + BLOCK] = substep(q0, b, parts)

    limit = limits[:1]

    def kept(at, step, shift):
        wave = step * (lax.broadcasted_iota(jnp.int32, (PIECE, 128), 0) + at) + shift
        return jnp.where(jnp.minimum(wave, NLON - wave) <= limit, 1.0 / NLON, 0.0)

    def products():
        odd_out[...] = jnp.dot(table[:, :NLON], odd_in[...], preferred_element_type=jnp.float32)
        even_out[...] = jnp.dot(table[:QUARTER, NLON:], even_in[...], preferred_element_type=jnp.float32)
        rest_out[...] = jnp.dot(table[QUARTER:, NLON:], rest_in[...], preferred_element_type=jnp.float32)

    def result(ref, at):
        return ref[at:at + PIECE, :128] + ref[at:at + PIECE, 128:]

    def filtered(q, finish):
        for b in range(0, QUARTER, PIECE):
            x = [q[8 + QUARTER * n + b:8 + QUARTER * n + b + PIECE] for n in range(4)]
            split(odd_in, b, x[0] - x[2], HALF)
            split(odd_in, QUARTER + b, x[1] - x[3], HALF)
            here, there = x[0] + x[2], x[1] + x[3]
            split(even_in, b, here + there, QUARTER)
            split(rest_in, b, here - there, QUARTER)
        products()
        for b in range(0, HALF, PIECE):
            split(odd_in, b, result(odd_out, b) * kept(b, 2, 1), HALF)
        for b in range(0, QUARTER, PIECE):
            split(even_in, b, result(even_out, b) * kept(b, 4, 0), QUARTER)
            split(rest_in, b, result(rest_out, b) * kept(b, 4, 2), QUARTER)
        products()
        for b in range(0, QUARTER, PIECE):
            odd = result(odd_out, b), result(odd_out, QUARTER + b)
            even, rest = result(even_out, b), result(rest_out, b)
            both = even + rest, even - rest
            for n in range(2):
                finish(QUARTER * n + b, both[n] + odd[n])
                finish(HALF + QUARTER * n + b, both[n] - odd[n])

    place = low + lanes_of(PIECE) % SPAN
    polar = (place >= 0) & (place < POLAR)

    def finish_first(at, value):
        q1[8 + at:8 + at + PIECE] = jnp.where(polar, value, q1[8 + at:8 + at + PIECE])

    upper = lanes_of(PIECE) >= 64

    def finish_second(at, value):
        before = pltpu.roll(q1[8 + at:8 + at + PIECE], 64, 1)
        split(lanes_in, at, jnp.where(upper, before, value))

    filtered(q1, finish_first)
    q1[7:8] = q1[7 + NLON:8 + NLON]
    q1[8 + NLON:9 + NLON] = q1[8:9]
    for b in range(0, NLON, BLOCK):
        q0[8 + b:8 + b + BLOCK] = substep(q1, b, [coef[n, b:b + BLOCK] for n in range(5)])
    filtered(q0, finish_second)
    spot = (lanes_of(128) - (SHARE * group + 31 * lat)) & 127
    field, r = spot // SLOT, spot % SLOT - lat
    source = field * SPAN + jnp.where((r >= 0) & (r < SHARE), 2 + r, 64 + jnp.where(lat == 0, SPAN - 3, 2))
    q1[8:8 + NLON] = moved((jnp.where(field < FIELDS, source, -1),))
    third = ((lane24 - (SHARE * group + 31 * lat)) & 127) // (FIELDS * SLOT)
    sends = []
    for n in range(RING // 2):
        chunk = None
        for t in range(3):
            value = q1[pl.ds(8 + 2 * LON * n + t, 24, stride=3), :]
            value = pltpu.roll(value, FIELDS * SLOT * t, 1) if t > 0 else value
            chunk = value if chunk is None else jnp.where(third < t, chunk, value)
        back[24 * n:24 * n + 24] = chunk
        if n % 4 == 3:
            rows = pl.ds(24 * (n - 3), 96)
            sends.append(pltpu.make_async_copy(back.at[rows], out.at[rows], sems.at[n // 4]))
            sends[-1].start()
    for copy in sends:
        copy.wait()


def join_kernel(middle, weight, back, out, block, sems):
    lane8 = lanes_of(8)
    lane = lanes_of(12)

    def body(lat):
        place = (lane - 32 * lat) & 127
        polar = place < POLAR
        even = ((place % 12 < SHARE) & (place != POLAR)) | (place == 127)
        copies = []
        for f in range(FIELDS):
            rows = pl.ds(f * UNIT, UNIT)
            block[rows, :] = middle[rows, :]
            for level in range(LEVELS):
                base = 12 * GROUPS * level
                for t in range(3):
                    start = FIELDS * SLOT * t + SLOT * f
                    target = (lane8 - (start + 32 * lat)) & 127
                    parts = []
                    for k in range(0, 24, 8):
                        value = back[base + k:base + k + 8]
                        for n in range(1, 8):
                            value = jnp.where(target >= 12 * n, back[base + 24 * n + k:base + 24 * n + k + 8], value)
                        parts.append(jnp.where(target >= 112, back[base + k:base + k + 8], value))
                    acc = pltpu.roll(jnp.concatenate(parts, axis=0), (-start) % 128, 1)
                    value = jnp.where(even, acc[:12], acc[12:])
                    at = pl.ds(f * UNIT + t * STEP + level + 2 * LEVELS * lat, 12, stride=3 * STEP)
                    near = weight[pl.ds(level * (LON + 4) + t, 12, stride=3), :]
                    block[at, :] = jnp.where(polar, value, middle[at, :] + near * value)
            copies.append(pltpu.make_async_copy(block.at[rows], out.at[rows], sems.at[f]))
            copies[-1].start()
        for copy in copies:
            copy.wait()

    on_core(body)


VMEM = pl.BlockSpec(memory_space=pltpu.VMEM)
SMEM = pl.BlockSpec(memory_space=pltpu.SMEM)
ANY = pl.BlockSpec(memory_space=pl.ANY)


def call(kernel, name, specs, shapes, scratch, grant, flops, moved, out_specs=None):
    params = {} if grant is None else {"vmem_limit_bytes": grant * 2**20}
    return pl.pallas_call(
        kernel,
        name=name,
        in_specs=specs,
        out_specs=jax.tree.map(lambda _: VMEM, shapes) if out_specs is None else out_specs,
        out_shape=shapes,
        scratch_shapes=scratch,
        compiler_params=pltpu.CompilerParams(**params),
        cost_estimate=pl.CostEstimate(flops=flops, bytes_accessed=moved, transcendentals=0),
    )


def f32(*shape):
    return jax.ShapeDtypeStruct(shape, jnp.float32)


def on_device(state, cx, cy, cutoff):
    state, cx, cy = to_rows(state), to_rows(cx), to_rows(cy)
    results = (f32(RING, 24, 128), f32(UNITS * LON * LEVELS, 128), f32(2 * EDGE * UNITS, 128))
    chunks, window, edge = call(
        pack_kernel,
        "pack",
        [ANY] * 3,
        results,
        [
            pltpu.VMEM((UNITS * UNIT, 128), jnp.float32),
            pltpu.VMEM((LEVELS, 4, 24, 128), jnp.float32),
            pltpu.VMEM((LEVELS, 12, 24, 128), jnp.float32),
            *(pltpu.VMEM(result.shape, jnp.float32) for result in results),
            pltpu.SemaphoreType.DMA((UNITS + 6,)),
        ],
        None,
        4_000_000,
        2_000_000,
        (ANY,) * 3,
    )(state, cx, cy)
    chunks = lax.all_to_all(chunks, "lon", 0, 0, tiled=True)
    window = lax.ppermute(window, "lat", [(0, 1), (1, 0)])
    head, tail = call(
        edge_kernel, "edges", [VMEM] * 2, (f32(EDGE * UNITS, 128),) * 2, [], 4, 100_000, 1_000_000
    )(edge, window)
    west = lax.ppermute(tail, "lon", [(i, (i + 1) % RING) for i in range(RING)])
    east = lax.ppermute(head, "lon", [((i + 1) % RING, i) for i in range(RING)])
    table = jnp.asarray(hartley_tables())
    limits = call(
        limit_kernel,
        "limits",
        [ANY, ANY, SMEM],
        jax.ShapeDtypeStruct((8, 128), jnp.int32),
        [],
        4,
        100_000,
        1_000_000,
    )(head, table, cutoff)
    back = call(
        circle_kernel,
        "circle",
        [VMEM] * 3 + [ANY] * 2,
        f32(RING * 12, 128),
        [
            pltpu.VMEM((RING * 12, 128), jnp.float32),
            pltpu.VMEM((NLON + 16, 128), jnp.float32),
            pltpu.VMEM((NLON + 16, 128), jnp.float32),
            pltpu.VMEM((5, NLON, 128), jnp.float32),
            pltpu.VMEM((NLON + 8, 256), jnp.float32),
            *(pltpu.VMEM((rows, 256), jnp.bfloat16) for rows in (NLON, HALF, HALF)),
            *(pltpu.VMEM((rows, 256), jnp.float32) for rows in (HALF, QUARTER, QUARTER)),
            pltpu.VMEM((NLON, 256), jnp.bfloat16),
            pltpu.SemaphoreType.DMA((4,)),
        ],
        24,
        1_000_000_000,
        6_000_000,
        ANY,
    )(chunks, table, limits, west, east)
    middle, weight = call(
        middle_kernel,
        "middle",
        [VMEM] * 6,
        (f32(FIELDS * UNIT, 128), f32(LEVELS * (LON + 4), 128)),
        [pltpu.VMEM((LON + 4, LAT + 128), jnp.float32), pltpu.VMEM((5, LON + 4, LAT + 128), jnp.float32)],
        8,
        20_000_000,
        3_000_000,
    )(state, cx, cy, west, east, window)
    back = lax.all_to_all(back.reshape(RING, 3, 4, 128), "lon", 0, 0, tiled=True).reshape(RING * 12, 128)
    out = call(
        join_kernel,
        "join",
        [VMEM] * 3,
        f32(FIELDS * UNIT, 128),
        [pltpu.VMEM((FIELDS * UNIT, 128), jnp.float32), pltpu.SemaphoreType.DMA((FIELDS,))],
        6,
        4_000_000,
        2_000_000,
        ANY,
    )(middle, weight, back)
    return from_rows(out)


def solution(mesh):
    return jax.shard_map(
        on_device,
        mesh=mesh,
        in_specs=(
            P(None, "lev", "lon", "lat"),
            P("lev", "lon", "lat"),
            P("lev", "lon", "lat"),
            P(),
        ),
        out_specs=P(None, "lev", "lon", "lat"),
        check_vma=False,
    )
```

```python
import math

import jax
import jax.numpy as jnp
import numpy as np
from jax import lax
from jax.experimental import pallas as pl
from jax.experimental.layout import Layout, with_layout_constraint
from jax.experimental.pallas import tpu as pltpu
from jax.sharding import PartitionSpec as P

FIELDS = 6
UNITS = 8
NLON = 1152
HALF = NLON // 2
QUARTER = NLON // 4
NLAT = 768
POLAR = 96
LEVELS = 2
LON = 36
LAT = 384
RING = 32
GROUPS = 16
SHARE = 6
SPAN = 10
SLOT = 7
KAPPA = 0.125
BLOCK = 64
PIECE = 48
TILES = LAT // 128
STEP = TILES * LEVELS
UNIT = LON * STEP
EDGE = 2 * STEP + 2 * LEVELS
ORDER = Layout(major_to_minor=(0, 1, 3, 2, 4))


def lanes_of(rows, width=128):
    return lax.broadcasted_iota(jnp.int32, (rows, width), 1)


def pick(flag, rows, width, yes, no):
    return jnp.where(jnp.full((rows, width), flag, jnp.int32) == 0, yes, no)


def to_rows(x):
    units = x.size // (LEVELS * LON * LAT)
    x = x.reshape(units, LEVELS, LON, LAT).transpose(0, 2, 1, 3)
    x = with_layout_constraint(x.reshape(units, LON, LEVELS, TILES, 128), ORDER)
    return x.transpose(0, 1, 3, 2, 4).reshape(units * UNIT, 128)


def from_rows(x):
    x = x.reshape(FIELDS, LON, TILES, LEVELS, 128).transpose(0, 1, 3, 2, 4)
    x = with_layout_constraint(x, ORDER)
    return x.reshape(FIELDS, LON, LEVELS, LAT).transpose(0, 2, 1, 3)


def unit(state, cx, cy, u):
    return (state, u * UNIT) if u < FIELDS else ((cx, cy)[u - FIELDS], 0)


def part(ref, start, level, tile, first, count):
    return ref[pl.ds(start + first * STEP + tile * LEVELS + level, count, stride=STEP), :]


def on_core(body):
    lat = lax.axis_index("lat")
    for n in range(2):
        pl.when(lat == n)(lambda n=n: body(n))


def pack_kernel(state, cx, cy, chunks_out, window_out, edge_out, block, tails, slots, chunks, window, edge, sems):
    loads = []
    for u in range(UNITS):
        ref, start = unit(state, cx, cy, u)
        loads.append(pltpu.make_async_copy(ref.at[start:start + UNIT], block.at[u * UNIT:u * UNIT + UNIT], sems.at[u]))
    for copy in loads:
        copy.start()
    sends = [
        pltpu.make_async_copy(window, window_out, sems.at[UNITS]),
        pltpu.make_async_copy(edge, edge_out, sems.at[UNITS + 1]),
    ]
    for n in range(4):
        some = pl.ds(n * RING // 4, RING // 4)
        sends.append(pltpu.make_async_copy(chunks.at[some], chunks_out.at[some], sems.at[UNITS + 2 + n]))
    lane = lanes_of(8)

    def body(lat):
        for u in range(UNITS):
            loads[u].wait()
            start = u * UNIT
            edge[EDGE * u:EDGE * u + EDGE] = block[start:start + EDGE]
            at = EDGE * (UNITS + u)
            edge[at:at + 12] = block[start + UNIT - 12:start + UNIT]
            edge[at + 12:at + EDGE] = block[start + UNIT - 4:start + UNIT]
            for level in range(LEVELS):
                rows = pl.ds(2 * LON * u + level, LON, stride=LEVELS)
                window[rows, :] = part(block, start, level, 2 - 2 * lat, 0, LON)
                main = part(block, start, level, 2 * lat, 0, 24)
                slots[level, u] = pltpu.roll(main, (SPAN * u - 32 * lat) % 128, 1)
                row = 12 * (u // 4)
                tails[level, u % 4, row:row + 12] = part(block, start, level, 2 * lat, 24, 12)
        sends[0].start()
        sends[1].start()
        for level in range(LEVELS):
            for at in range(4):
                slots[level, 8 + at] = pltpu.roll(tails[level, at], (SPAN * (8 + at) - 32 * lat) % 128, 1)
            for g in range(GROUPS):
                first = SHARE * g - 2
                begins = sorted(((first + SPAN * n) % 128, n) for n in range(12))
                for k in range(0, 24, 8):
                    value = slots[level, begins[-1][1], k:k + 8]
                    for begin, n in begins:
                        value = jnp.where(lane >= begin, slots[level, n, k:k + 8], value)
                    chunks[level * GROUPS + g, k:k + 8] = value
                if g % 8 == 7:
                    sends[2 + level * 2 + g // 8].start()

    on_core(body)
    for copy in sends:
        copy.wait()


def edge_kernel(edge, window, head, tail):
    head[...] = edge[:EDGE * UNITS]
    tail[...] = edge[EDGE * UNITS:]
    for u in range(UNITS):
        at, beyond = EDGE * u, 2 * LON * u
        head[at + 12:at + EDGE] = window[beyond:beyond + 4]
        tail[at + 12:at + EDGE] = window[beyond + 2 * LON - 4:beyond + 2 * LON]


def limit_kernel(head, table, cutoff, limits):
    del head, table
    low = lax.axis_index("lat") * (NLAT - POLAR) + SHARE * lax.rem(lax.axis_index("lon"), GROUPS) - 2
    row = lanes_of(8) % SPAN
    found = jnp.zeros((8, 128), jnp.int32)
    for r in range(SPAN):
        found = jnp.where(row == r, cutoff[jnp.clip(low + r, 0, NLAT - 1)], found)
    limits[...] = found


def coefficients(cx, cx_east, cy_south, cy_north):
    west = jnp.maximum(cx, 0.0) + KAPPA
    east = KAPPA - jnp.minimum(cx_east, 0.0)
    south = jnp.maximum(cy_south, 0.0) + KAPPA
    north = KAPPA - jnp.minimum(cy_north, 0.0)
    centre = (
        (1.0 - 4.0 * KAPPA)
        + (jnp.minimum(cx, 0.0) - jnp.maximum(cx_east, 0.0))
        + (jnp.minimum(cy_south, 0.0) - jnp.maximum(cy_north, 0.0))
    )
    return west, east, south, north, centre


def middle_kernel(state, cx, cy, west, east, window, out, weight, ext, coef):
    lat = lax.axis_index("lat")

    def extended(u, level):
        ref, start = unit(state, cx, cy, u)
        for t in range(TILES):
            ext[:LON, 128 * t:128 * t + 128] = part(ref, start, level, t, 0, LON)
            ext[LON:LON + 2, 128 * t:128 * t + 128] = part(east, EDGE * u, level, t, 0, 2)
            ext[LON + 2:, 128 * t:128 * t + 128] = part(west, EDGE * u, level, t, 0, 2)
        ext[:LON, LAT:] = window[pl.ds(2 * LON * u + level, LON, stride=LEVELS), :]
        ext[LON:LON + 2, LAT:] = east[pl.ds(EDGE * u + 12 + level, 2, stride=LEVELS), :]
        ext[LON + 2:, LAT:] = west[pl.ds(EDGE * u + 12 + level, 2, stride=LEVELS), :]
        return ext[...]

    lane = lanes_of(LON + 4, LAT + 128)
    edge = lane == jnp.where(lat == 0, POLAR - 1, LAT - POLAR)
    beside = lanes_of(LON + 4) == jnp.where(lat == 0, POLAR, 31)
    for level in range(LEVELS):
        cxe = extended(FIELDS, level)
        cye = extended(FIELDS + 1, level)
        parts = coefficients(cxe, pltpu.roll(cxe, LON + 3, 0), pltpu.roll(cye, 1, 1), cye)
        for n, value in enumerate(parts):
            coef[n] = value
        near = pick(lat, LON + 4, 128, parts[2][:, :128], parts[3][:, 256:LAT])
        weight[level * (LON + 4):(level + 1) * (LON + 4)] = jnp.where(beside, near, 0.0)

        def substep(q):
            return (
                coef[0] * pltpu.roll(q, 1, 0)
                + coef[1] * pltpu.roll(q, LON + 3, 0)
                + coef[2] * pltpu.roll(q, 1, 1)
                + coef[3] * pltpu.roll(q, LAT + 127, 1)
                + coef[4] * q
            )

        for u in range(FIELDS):
            once = jnp.where(edge, 0.0, substep(extended(u, level)))
            twice = substep(once)
            for t in range(TILES):
                rows = pl.ds(u * UNIT + t * LEVELS + level, LON, stride=STEP)
                out[rows, :] = twice[:LON, 128 * t:128 * t + 128]


def hartley_tables():
    def split(n, shift):
        at = 2 * np.arange(n, dtype=np.int64) + shift
        angle = 2.0 * np.pi / (4 * n) * (at[:, None] * at[None, :] % (4 * n))
        table = np.cos(angle) + np.sin(angle)
        high = table.astype(jnp.bfloat16)
        low = (table - high.astype(np.float64)).astype(jnp.bfloat16)
        return np.concatenate([high, low], axis=1)

    even = np.concatenate([split(QUARTER, 0), split(QUARTER, 1)], axis=0)
    return np.concatenate([split(HALF, 1), even], axis=1)


def circle_kernel(chunks, table, limits, west, east, out, back, q0, q1, coef, spread, *buffers):
    del west, east
    odd_in, even_in, rest_in, odd_out, even_out, rest_out, lanes_in, sems = buffers
    lat = lax.axis_index("lat")
    group = lax.rem(lax.axis_index("lon"), GROUPS)
    low = SHARE * group - 2
    lane24 = lanes_of(24)
    for i in range(RING):
        chunk = chunks[i]
        at = 8 + LON * i
        q0[at:at + 24] = pltpu.roll(chunk, (-low) & 127, 1)
        upper = pltpu.roll(chunk, (-low - 8 * SPAN) & 127, 1)
        lower = pltpu.roll(chunk, (-low - 4 * SPAN) & 127, 1)
        q0[at + 24:at + 36] = jnp.where(lane24[:12] < 4 * SPAN, upper[:12], lower[12:])
    q0[7:8] = q0[7 + NLON:8 + NLON]
    q0[8 + NLON:9 + NLON] = q0[8:9]

    row = lanes_of(BLOCK) % SPAN
    pole_south = (row == 2) & (jnp.full((BLOCK, 128), lat + group, jnp.int32) == 0)
    pole_north = (row == SPAN - 3) & (jnp.full((BLOCK, 128), lat * GROUPS + group, jnp.int32) == 2 * GROUPS - 1)

    def split(ref, at, x, again=0):
        rows = x.shape[0]
        high = x.astype(jnp.bfloat16)
        rest = (x - high.astype(jnp.float32)).astype(jnp.bfloat16)
        for begin in (at, at + again)[:2 if again else 1]:
            ref[begin:begin + rows, :128] = high
            ref[begin:begin + rows, 128:] = rest

    def moved(sources):
        at = lax.broadcasted_iota(jnp.int32, (128, 128), 0)
        places = [jnp.where(at == source, 1.0, 0.0).astype(jnp.bfloat16) for source in sources]
        places = jnp.concatenate(places, axis=1)
        return jnp.dot(lanes_in[...], jnp.concatenate([places] * 2, axis=0), preferred_element_type=jnp.float32)

    for b in range(0, NLON, PIECE):
        split(lanes_in, b, q0[8 + b:8 + b + PIECE])
    take_x = FIELDS * SPAN + lanes_of(128) % SPAN
    spread[:NLON] = moved((take_x, take_x + SPAN))
    spread[NLON:NLON + 8] = spread[:8]

    def substep(q, b, parts):
        across = q[8 + (b + HALF) % NLON:8 + (b + HALF) % NLON + BLOCK]
        here = q[8 + b:8 + b + BLOCK]
        return (
            parts[0] * q[7 + b:7 + b + BLOCK]
            + parts[1] * q[9 + b:9 + b + BLOCK]
            + parts[2] * jnp.where(pole_south, across, pltpu.roll(here, 1, 1))
            + parts[3] * jnp.where(pole_north, across, pltpu.roll(here, 127, 1))
            + parts[4] * here
        )

    for b in range(0, NLON, BLOCK):
        cy = spread[b:b + BLOCK, 128:]
        parts = coefficients(
            spread[b:b + BLOCK, :128],
            spread[b + 1:b + 1 + BLOCK, :128],
            jnp.where(pole_south, 0.0, pltpu.roll(cy, 1, 1)),
            jnp.where(pole_north, 0.0, cy),
        )
        for n, value in enumerate(parts):
            coef[n, b:b + BLOCK] = value
        q1[8 + b:8 + b + BLOCK] = substep(q0, b, parts)

    limit = limits[:1]

    def kept(at, step, shift):
        wave = step * (lax.broadcasted_iota(jnp.int32, (PIECE, 128), 0) + at) + shift
        return jnp.where(jnp.minimum(wave, NLON - wave) <= limit, 1.0 / NLON, 0.0)

    parts = {
        "odd": (odd_in, odd_out, HALF, (2, 1), (slice(None), slice(0, NLON))),
        "even": (even_in, even_out, QUARTER, (4, 0), (slice(0, QUARTER), slice(NLON, None))),
        "rest": (rest_in, rest_out, QUARTER, (4, 2), (slice(QUARTER, None), slice(NLON, None))),
    }

    def product(name):
        source, target, _, _, place = parts[name]
        target[...] = jnp.dot(table[place], source[...], preferred_element_type=jnp.float32)

    def cut(name):
        source, target, count, waves, _ = parts[name]
        for b in range(0, count, PIECE):
            split(source, b, result(target, b) * kept(b, *waves), count)

    def result(ref, at):
        return ref[at:at + PIECE, :128] + ref[at:at + PIECE, 128:]

    def filtered(q, finish):
        for b in range(0, HALF, PIECE):
            split(odd_in, b, q[8 + b:8 + b + PIECE] - q[8 + HALF + b:8 + HALF + b + PIECE], HALF)
        product("odd")
        for b in range(0, QUARTER, PIECE):
            x = [q[8 + QUARTER * n + b:8 + QUARTER * n + b + PIECE] for n in range(4)]
            here, there = x[0] + x[2], x[1] + x[3]
            split(even_in, b, here + there, QUARTER)
            split(rest_in, b, here - there, QUARTER)
        product("even")
        product("rest")
        for name in parts:
            cut(name)
            product(name)
        for b in range(0, QUARTER, PIECE):
            odd = result(odd_out, b), result(odd_out, QUARTER + b)
            even, rest = result(even_out, b), result(rest_out, b)
            both = even + rest, even - rest
            for n in range(2):
                finish(QUARTER * n + b, both[n] + odd[n])
                finish(HALF + QUARTER * n + b, both[n] - odd[n])

    place = low + lanes_of(PIECE) % SPAN
    polar = (place >= 0) & (place < POLAR)

    def finish_first(at, value):
        q1[8 + at:8 + at + PIECE] = jnp.where(polar, value, q1[8 + at:8 + at + PIECE])

    upper = lanes_of(PIECE) >= 64

    def finish_second(at, value):
        before = pltpu.roll(q1[8 + at:8 + at + PIECE], 64, 1)
        split(lanes_in, at, jnp.where(upper, before, value))

    filtered(q1, finish_first)
    q1[7:8] = q1[7 + NLON:8 + NLON]
    q1[8 + NLON:9 + NLON] = q1[8:9]
    for b in range(0, NLON, BLOCK):
        q0[8 + b:8 + b + BLOCK] = substep(q1, b, [coef[n, b:b + BLOCK] for n in range(5)])
    filtered(q0, finish_second)
    spot = (lanes_of(128) - (SHARE * group + 31 * lat)) & 127
    field, r = spot // SLOT, spot % SLOT - lat
    source = field * SPAN + jnp.where((r >= 0) & (r < SHARE), 2 + r, 64 + jnp.where(lat == 0, SPAN - 3, 2))
    q1[8:8 + NLON] = moved((jnp.where(field < FIELDS, source, -1),))
    third = ((lane24 - (SHARE * group + 31 * lat)) & 127) // (FIELDS * SLOT)
    sends = []
    for n in range(RING // 2):
        chunk = None
        for t in range(3):
            value = q1[pl.ds(8 + 2 * LON * n + t, 24, stride=3), :]
            value = pltpu.roll(value, FIELDS * SLOT * t, 1) if t > 0 else value
            chunk = value if chunk is None else jnp.where(third < t, chunk, value)
        back[24 * n:24 * n + 24] = chunk
        if n % 4 == 3:
            rows = pl.ds(24 * (n - 3), 96)
            sends.append(pltpu.make_async_copy(back.at[rows], out.at[rows], sems.at[n // 4]))
            sends[-1].start()
    for copy in sends:
        copy.wait()


def join_kernel(middle, weight, back, out, block, sems):
    lane8 = lanes_of(8)
    lane = lanes_of(12)

    def body(lat):
        place = (lane - 32 * lat) & 127
        polar = place < POLAR
        even = ((place % 12 < SHARE) & (place != POLAR)) | (place == 127)
        copies = []
        for f in range(FIELDS):
            rows = pl.ds(f * UNIT, UNIT)
            block[rows, :] = middle[rows, :]
            for level in range(LEVELS):
                base = 12 * GROUPS * level
                for t in range(3):
                    start = FIELDS * SLOT * t + SLOT * f
                    target = (lane8 - (start + 32 * lat)) & 127
                    parts = []
                    for k in range(0, 24, 8):
                        value = back[base + k:base + k + 8]
                        for n in range(1, 8):
                            value = jnp.where(target >= 12 * n, back[base + 24 * n + k:base + 24 * n + k + 8], value)
                        parts.append(jnp.where(target >= 112, back[base + k:base + k + 8], value))
                    acc = pltpu.roll(jnp.concatenate(parts, axis=0), (-start) % 128, 1)
                    value = jnp.where(even, acc[:12], acc[12:])
                    at = pl.ds(f * UNIT + t * STEP + level + 2 * LEVELS * lat, 12, stride=3 * STEP)
                    near = weight[pl.ds(level * (LON + 4) + t, 12, stride=3), :]
                    block[at, :] = jnp.where(polar, value, middle[at, :] + near * value)
            copies.append(pltpu.make_async_copy(block.at[rows], out.at[rows], sems.at[f]))
            copies[-1].start()
        for copy in copies:
            copy.wait()

    on_core(body)


VMEM = pl.BlockSpec(memory_space=pltpu.VMEM)
SMEM = pl.BlockSpec(memory_space=pltpu.SMEM)
ANY = pl.BlockSpec(memory_space=pl.ANY)


def call(kernel, name, specs, shapes, scratch, grant, flops, moved, out_specs=None):
    params = {} if grant is None else {"vmem_limit_bytes": grant * 2**20}
    return pl.pallas_call(
        kernel,
        name=name,
        in_specs=specs,
        out_specs=jax.tree.map(lambda _: VMEM, shapes) if out_specs is None else out_specs,
        out_shape=shapes,
        scratch_shapes=scratch,
        compiler_params=pltpu.CompilerParams(**params),
        cost_estimate=pl.CostEstimate(flops=flops, bytes_accessed=moved, transcendentals=0),
    )


def f32(*shape):
    return jax.ShapeDtypeStruct(shape, jnp.float32)


def on_device(state, cx, cy, cutoff):
    state, cx, cy = to_rows(state), to_rows(cx), to_rows(cy)
    results = (f32(RING, 24, 128), f32(UNITS * LON * LEVELS, 128), f32(2 * EDGE * UNITS, 128))
    chunks, window, edge = call(
        pack_kernel,
        "pack",
        [ANY] * 3,
        results,
        [
            pltpu.VMEM((UNITS * UNIT, 128), jnp.float32),
            pltpu.VMEM((LEVELS, 4, 24, 128), jnp.float32),
            pltpu.VMEM((LEVELS, 12, 24, 128), jnp.float32),
            *(pltpu.VMEM(result.shape, jnp.float32) for result in results),
            pltpu.SemaphoreType.DMA((UNITS + 6,)),
        ],
        None,
        4_000_000,
        2_000_000,
        (ANY,) * 3,
    )(state, cx, cy)
    chunks = lax.all_to_all(chunks, "lon", 0, 0, tiled=True)
    window = lax.ppermute(window, "lat", [(0, 1), (1, 0)])
    head, tail = call(
        edge_kernel, "edges", [VMEM] * 2, (f32(EDGE * UNITS, 128),) * 2, [], 4, 100_000, 1_000_000
    )(edge, window)
    west = lax.ppermute(tail, "lon", [(i, (i + 1) % RING) for i in range(RING)])
    east = lax.ppermute(head, "lon", [((i + 1) % RING, i) for i in range(RING)])
    table = jnp.asarray(hartley_tables())
    limits = call(
        limit_kernel,
        "limits",
        [ANY, ANY, SMEM],
        jax.ShapeDtypeStruct((8, 128), jnp.int32),
        [],
        4,
        100_000,
        1_000_000,
    )(head, table, cutoff)
    back = call(
        circle_kernel,
        "circle",
        [VMEM] * 3 + [ANY] * 2,
        f32(RING * 12, 128),
        [
            pltpu.VMEM((RING * 12, 128), jnp.float32),
            pltpu.VMEM((NLON + 16, 128), jnp.float32),
            pltpu.VMEM((NLON + 16, 128), jnp.float32),
            pltpu.VMEM((5, NLON, 128), jnp.float32),
            pltpu.VMEM((NLON + 8, 256), jnp.float32),
            *(pltpu.VMEM((rows, 256), jnp.bfloat16) for rows in (NLON, HALF, HALF)),
            *(pltpu.VMEM((rows, 256), jnp.float32) for rows in (HALF, QUARTER, QUARTER)),
            pltpu.VMEM((NLON, 256), jnp.bfloat16),
            pltpu.SemaphoreType.DMA((4,)),
        ],
        24,
        1_000_000_000,
        6_000_000,
        ANY,
    )(chunks, table, limits, west, east)
    middle, weight = call(
        middle_kernel,
        "middle",
        [VMEM] * 6,
        (f32(FIELDS * UNIT, 128), f32(LEVELS * (LON + 4), 128)),
        [pltpu.VMEM((LON + 4, LAT + 128), jnp.float32), pltpu.VMEM((5, LON + 4, LAT + 128), jnp.float32)],
        8,
        20_000_000,
        3_000_000,
    )(state, cx, cy, west, east, window)
    back = lax.all_to_all(back.reshape(RING, 3, 4, 128), "lon", 0, 0, tiled=True).reshape(RING * 12, 128)
    out = call(
        join_kernel,
        "join",
        [VMEM] * 3,
        f32(FIELDS * UNIT, 128),
        [pltpu.VMEM((FIELDS * UNIT, 128), jnp.float32), pltpu.SemaphoreType.DMA((FIELDS,))],
        6,
        4_000_000,
        2_000_000,
        ANY,
    )(middle, weight, back)
    return from_rows(out)


def solution(mesh):
    return jax.shard_map(
        on_device,
        mesh=mesh,
        in_specs=(
            P(None, "lev", "lon", "lat"),
            P("lev", "lon", "lat"),
            P("lev", "lon", "lat"),
            P(),
        ),
        out_specs=P(None, "lev", "lon", "lat"),
        check_vma=False,
    )
```
